32 devices in a mesh: groups: 2 (over y), chain: 4 (over x, core), sector: 4 (over z).
Axes of the slice: x: 2, y: 2, z: 4, core: 2. Of those that a mesh axis runs over, the one named last changes fastest.
Arguments:
- psi_first: bfloat16 [8, 4, 64, 1024], P(('groups', 'chain'), 'sector'), parts along dimension 0, may hold values from -6 to 6
- psi_second: bfloat16 [8, 4, 64, 1024], P(('groups', 'chain'), 'sector'), parts along dimension 0, may hold values from -6 to 6
- left_env: bfloat16 [8, 4, 64, 1664], P(('groups', 'chain'), 'sector'), parts along dimension 0, may hold values from -0.15625 to 0.15625
- right_env: bfloat16 [8, 4, 64, 1664], P(('groups', 'chain'), 'sector'), parts along dimension 0, may hold values from -0.75 to 0.75
- site_tensor: bfloat16 [8, 4, 64, 256], P(('groups', 'chain'), 'sector'), parts along dimension 0, may hold values from -3 to 3
- mpo: bfloat16 [8, 2, 26, 26, 16], P(('groups', 'chain')), parts along dimension 0, may hold values from -0.625 to 0.625
- mpo_pattern: int32 [8, 2, 26, 26], P(('groups', 'chain')), parts along dimension 0, may hold values 0 or 1
- sector_labels: int32 [8, 26, 4], P(('groups', 'chain'), None, 'sector'), parts along dimension 0, may hold values from 0 to 3, as said below
- live_sizes: int32 [8, 4], P(('groups', 'chain'), 'sector'), parts along dimension 0, may hold values from 32 to 64, as said below
Outputs:
- sigma_first: bfloat16 [8, 4, 64, 1024], P(('groups', 'chain'), 'sector'), parts along dimension 0
- sigma_second: bfloat16 [8, 4, 64, 1024], P(('groups', 'chain'), 'sector'), parts along dimension 0
- next_env: bfloat16 [8, 4, 64, 1664], P(('groups', 'chain'), 'sector'), parts along dimension 0
The draws below stay inside these ranges and needn't reach their ends.
There are 2 independent parts, one for each index of `groups`. The reference program is written for one: setup_inputs(seed, part) draws one part's arguments, and reference() takes and returns one part's arrays. A program takes and returns all parts, laid end to end along the dimension named above; each array names one. Nothing has to cross between parts.
Inputs may be any that keep to these rules, and one draw needn't show every extreme that they name: `live_sizes`: in every site some sector has all 64 states live. Sector q stands at spin-up count q % (2) and spin-down count q // 2 on a periodic grid of 2 by 2 charges. Each channel x of a site carries one charge shift of 0, +1 or -1 up, +1 or -1 down (channels 0 and 25 carry 0), and sector_labels[j, x, q] is the sector at the charge of q plus that shift, wrapped on the grid.
All inputs are finite; a program needn't handle non-finite values. No bound on the sum of `mpo_pattern` on one device may be relied on, other than what follows from the above.
Results may differ from the reference program's by a relative error of at most 0.008.
Values may be sent and summed in bfloat16 or wider, within the bound.
A program may use at most 128 MiB of HBM per device.

```python
import jax
import jax.numpy as jnp
from jax import lax

BLOCK = 64
MPO_BOND = 26
LOCAL = 4
SEC_DEV = 1
PAIR = 16
SECTORS = 4
SITES = 4
N_SECTOR = 4


def draw_live_sizes(key, part):
    key = jax.random.fold_in(key, 7)
    first_key, second_key = jax.random.split(key)
    live_sizes = jax.random.randint(first_key, (SITES, SECTORS), BLOCK // 2, BLOCK + 1)
    fullest = jax.random.randint(second_key, (SITES,), 0, SECTORS)
    columns = jnp.arange(SECTORS)[None, :]
    live_sizes = jnp.where(columns == fullest[:, None], BLOCK, live_sizes)
    return live_sizes.astype(jnp.int32)


def draw_sector_labels(key, part):
    key = jax.random.fold_in(key, 11)
    shifts = jax.random.randint(key, (SITES, MPO_BOND), 0, 5).astype(jnp.int32)
    channels = jnp.arange(MPO_BOND).astype(jnp.int32)[None, :]
    edges = (channels == 0) | (channels == MPO_BOND - 1)
    shifts = jnp.where(edges, 0, shifts)
    up_table = jnp.array([0, 1, -1, 0, 0], jnp.int32)
    down_table = jnp.array([0, 0, 0, 1, -1], jnp.int32)
    up_shift = up_table[shifts][:, :, None]
    down_shift = down_table[shifts][:, :, None]
    sector = jnp.arange(SECTORS).astype(jnp.int32)[None, None, :]
    up_count = SECTORS // 2
    up_charge = (sector % up_count + up_shift) % up_count
    down_charge = (sector // up_count + down_shift) % 2
    return (down_charge * up_count + up_charge).astype(jnp.int32)


def touch_ends(drawn, key, low, top_value):
    extent = drawn.shape
    index_at = [jax.random.randint(jax.random.fold_in(key, axis), (), 0, extent[axis]) for axis in range(len(extent))]
    drawn = drawn.at[tuple(index_at)].set(low)
    longest = extent.index(max(extent))
    index_at[longest] = (index_at[longest] + 1) % extent[longest]
    return drawn.at[tuple(index_at)].set(top_value)


def levels(own_key, shape, cuts, smallest, largest):
    loudness, own = 1.0, jax.random.fold_in(own_key, 6)
    for position, shards_of in cuts:
        draws = jnp.exp(jax.random.uniform(jax.random.fold_in(own, position), (shards_of,), jnp.float32, smallest / len(cuts), largest / len(cuts)))
        loudness = loudness * jnp.repeat(draws, shape[position] // shards_of).reshape([-1 if axis == position else 1 for axis in range(len(shape))])
    return loudness


def noise(rng, shape, scale, reach, pieces=(), kind=jnp.bfloat16):
    result = jax.random.normal(rng, shape, jnp.float32) * scale
    if len(pieces) > 0:
        result = levels(rng, shape, pieces, -0.22, 0.18) * result
    return jnp.clip(result, min=-reach, max=reach).astype(kind)


def setup_inputs(seed: int = 0, part: int = 0) -> dict:
    key_list = jax.random.split(jax.random.key(seed), 10)
    part_keys = jax.random.split(jax.random.fold_in(key_list[9], part), 10)
    return {
        "psi_first": noise(part_keys[0], (SITES, SECTORS, BLOCK, PAIR * BLOCK), 1.0, 6.0, ((0, 4), (1, 4))),
        "psi_second": noise(part_keys[1], (SITES, SECTORS, BLOCK, PAIR * BLOCK), 1.0, 6.0, ((0, 4), (1, 4))),
        "left_env": noise(part_keys[2], (SITES, SECTORS, BLOCK, MPO_BOND * BLOCK), (BLOCK * MPO_BOND) ** -0.5, 0.15625, ((0, 4), (1, 4))),
        "right_env": noise(part_keys[3], (SITES, SECTORS, BLOCK, MPO_BOND * BLOCK), BLOCK ** -0.5, 0.75, ((0, 4), (1, 4))),
        "site_tensor": noise(part_keys[4], (SITES, SECTORS, BLOCK, LOCAL * BLOCK), 0.5, 3.0, ((0, 4), (1, 4))),
        "mpo": noise(part_keys[5], (SITES, 2, MPO_BOND, MPO_BOND, PAIR), (MPO_BOND * LOCAL) ** -0.5, 0.625, ((0, 4),)),
        "mpo_pattern": touch_ends((jax.random.randint(part_keys[6], (SITES, 2, MPO_BOND, MPO_BOND), 0, 4) < 3).astype(jnp.int32), jax.random.fold_in(part_keys[6], 1), 0, 1),
        "sector_labels": draw_sector_labels(jax.random.fold_in(jax.random.fold_in(key_list[9], part), 71), part),
        "live_sizes": draw_live_sizes(jax.random.fold_in(jax.random.fold_in(key_list[9], part), 71), part),
    }


def sector_terms(psis, right_block, left_block, first_site, second_site, labels, partial_value):
    right_part = right_block.reshape(BLOCK, MPO_BOND, BLOCK).astype(jnp.float32)
    section_one = jnp.einsum('pwc,nastc->nwastp', right_part, psis.astype(jnp.float32)).astype(jnp.bfloat16)
    section_two = jnp.einsum('vwut,nwastp->nvasup', second_site.astype(jnp.float32), section_one.astype(jnp.float32)).astype(jnp.bfloat16)
    section_three = jnp.einsum('xvrs,nvasup->xnarup', first_site.astype(jnp.float32), section_two.astype(jnp.float32)).astype(jnp.bfloat16)
    section_three = section_three.reshape(MPO_BOND, 2, BLOCK, PAIR * BLOCK)
    left_part = jnp.moveaxis(left_block.reshape(BLOCK, MPO_BOND, BLOCK), 1, 0)

    def add_term(carry, operands):
        left_slice, upper, target = operands
        product = jnp.einsum('ba,naz->nbz', left_slice.astype(jnp.float32), upper.astype(jnp.float32))
        target = target.astype(jnp.int32)
        current = lax.dynamic_slice_in_dim(carry, target, 1, 1)
        return lax.dynamic_update_slice_in_dim(carry, current + product[:, None], target, 1), None

    return lax.scan(add_term, partial_value, (left_part, section_three, labels))[0]


def one_site(operands):
    first_psi, second_psi, left_env, right_env, tensor, weights, pattern, labels, live_sizes = operands
    kept = (jnp.arange(BLOCK).astype(jnp.int32)[None, :] < live_sizes[:, None]).astype(jnp.bfloat16)
    psis = jnp.stack([first_psi, second_psi]).reshape(2, SECTORS, BLOCK, LOCAL, LOCAL, BLOCK)
    psis = psis * kept[None, :, :, None, None, None] * kept[None, :, None, None, None, :]
    masked = (weights * pattern[..., None].astype(weights.dtype)).reshape(2, MPO_BOND, MPO_BOND, LOCAL, LOCAL)
    zeros = jnp.zeros((2, SECTORS, BLOCK, PAIR * BLOCK), jnp.float32)

    def device_sum(summed, member):
        def sector_step(partial_value, sector):
            return sector_terms(psis[:, sector], right_env[sector], left_env[sector], masked[0], masked[1], labels[:, sector], partial_value), None

        owned = member * SEC_DEV + jnp.arange(SEC_DEV).astype(jnp.int32)
        partial_value = lax.scan(sector_step, zeros, owned)[0]
        rounded = lax.optimization_barrier(partial_value.astype(jnp.bfloat16))
        return summed + rounded.astype(jnp.float32), None

    summed = lax.scan(device_sum, zeros, jnp.arange(N_SECTOR).astype(jnp.int32))[0]
    kept_float = kept.astype(jnp.float32)
    summed = summed.reshape(2, SECTORS, BLOCK, PAIR, BLOCK) * kept_float[None, :, :, None, None] * kept_float[None, :, None, None, :]
    sigmas = summed.reshape(2, SECTORS, BLOCK, PAIR * BLOCK).astype(jnp.bfloat16)

    site_part = tensor.reshape(SECTORS, BLOCK, LOCAL, BLOCK) * kept[:, :, None, None] * kept[:, None, None, :]
    left_part = left_env.reshape(SECTORS, BLOCK, MPO_BOND, BLOCK).astype(jnp.float32)
    env_one = jnp.einsum('qbwa,qasc->qwbsc', left_part, site_part.astype(jnp.float32)).astype(jnp.bfloat16)
    bra = site_part[jnp.transpose(labels).astype(jnp.int32)]
    env_two = jnp.einsum('qwbre,qwbsc->qwresc', bra.astype(jnp.float32), env_one.astype(jnp.float32)).astype(jnp.bfloat16)
    updated = jnp.einsum('wvrs,qwresc->qevc', masked[0].astype(jnp.float32), env_two.astype(jnp.float32)).astype(jnp.bfloat16)
    return sigmas[0], sigmas[1], updated.reshape(SECTORS, BLOCK, MPO_BOND * BLOCK)


def reference(psi_first, psi_second, left_env, right_env, site_tensor, mpo, mpo_pattern, sector_labels, live_sizes):
    sigma_first, sigma_second, updated = lax.map(one_site, (psi_first, psi_second, left_env, right_env, site_tensor, mpo, mpo_pattern, sector_labels, live_sizes))
    next_env = jnp.concatenate([left_env[:1], updated[:-1]], axis=0)
    return sigma_first, sigma_second, next_env
```

```python
import functools

import jax
import jax.numpy as jnp
from jax import lax
from jax.experimental import pallas as pl
from jax.experimental.pallas import tpu as pltpu
from jax.sharding import PartitionSpec as P

ROWS = 32
BF16 = jnp.bfloat16
F32 = jnp.float32


def padded_operator(op, bond):
    op = jnp.transpose(op, (2, 0, 3, 1))
    op = jnp.pad(op, ((0, 0), (0, ROWS - bond), (0, 0), (0, ROWS - bond)))
    return op.reshape(op.shape[0] * ROWS, op.shape[2] * ROWS)


def halves(first, second, low):
    lane = lax.broadcasted_iota(jnp.int32, first.shape, 1)
    return jnp.where(lane < low, first, second)


def sigma_kernel(
    block, bond, local, live_ref, labels_ref, first_ref, second_ref, right_ref, left_ref, two_ref, one_ref,
    out_ref, psi_s, right_s, x_s, y_s, z_s, lk_s,
):
    wide = 2 * block
    pair = local * local
    sectors = out_ref.shape[0]
    live = live_ref[0, 0]
    row = lax.broadcasted_iota(jnp.int32, (block, wide), 0)
    lane = lax.broadcasted_iota(jnp.int32, (block, wide), 1)
    keep = (row < live) & (lax.rem(lane, block) < live)
    for tile in range(pair // 2):
        at = slice(tile * wide, (tile + 1) * wide)
        a = first_ref[:, at].astype(F32)
        b = second_ref[:, at].astype(F32)
        even = jnp.where(lane < block, a, pltpu.roll(b, block, 1))
        odd = jnp.where(lane < block, pltpu.roll(a, block, 1), b)
        psi_s[pl.ds(2 * tile * block, block), :] = jnp.where(keep, even, 0.0).astype(BF16)
        psi_s[pl.ds((2 * tile + 1) * block, block), :] = jnp.where(keep, odd, 0.0).astype(BF16)
    for tile in range(bond // 2):
        a = right_ref[:, tile * wide : (tile + 1) * wide].astype(F32)
        swapped = pltpu.roll(a, block, 1)
        zero = jnp.zeros_like(a)
        right_s[pl.ds(tile * 2 * wide, block), :] = jnp.where(lane < block, a, zero).astype(BF16)
        right_s[pl.ds(tile * 2 * wide + block, block), :] = jnp.where(lane < block, zero, swapped).astype(BF16)
        right_s[pl.ds(tile * 2 * wide + wide, block), :] = jnp.where(lane < block, swapped, zero).astype(BF16)
        right_s[pl.ds(tile * 2 * wide + wide + block, block), :] = jnp.where(lane < block, zero, a).astype(BF16)
    for k in range(sectors):
        lk_s[pl.ds(k * block, block), :] = jnp.where(
            labels_ref[...] == k, left_ref[...].astype(F32), 0.0
        ).astype(BF16)
    stride = pair * ROWS

    def put(st, w, value):
        x_s[pl.ds(st * ROWS + w, block, stride=stride), :] = value

    for st in range(pair):
        for w in range(bond, ROWS):
            put(st, w, jnp.zeros((block, wide), F32))

    def one(st, carry):
        lhs = psi_s[pl.ds(pl.multiple_of(st * block, block), block), :]
        for tile in range(bond // 2):
            got = lax.dot_general(
                lhs, right_s[pl.ds(tile * 2 * wide, 2 * wide), :], (((1,), (1,)), ((), ())),
                preferred_element_type=F32,
            )
            put(st, 2 * tile, got[:, :wide])
            put(st, 2 * tile + 1, got[:, wide:])
        return carry

    lax.fori_loop(0, pair, one, 0)
    two = two_ref[...]
    rows = local * ROWS

    def middle(a, carry):
        x = x_s[pl.ds(pl.multiple_of(a * stride, stride), stride), :].astype(BF16)
        x = jnp.concatenate([x[s * rows : (s + 1) * rows] for s in range(local)], axis=1)
        y = jnp.dot(two, x, preferred_element_type=F32).astype(BF16)
        for u in range(local):
            for s in range(local):
                y_s[u, pl.ds(pl.multiple_of(a * rows, rows) + s * ROWS, ROWS), :] = y[
                    u * ROWS : (u + 1) * ROWS, s * wide : (s + 1) * wide
                ]
        return carry

    lax.fori_loop(0, block, middle, 0, unroll=2)
    op = one_ref[...]
    group = 4

    def last(u, carry):
        def third(step, carry):
            y = y_s[u, pl.ds(pl.multiple_of(step * group * rows, group * rows), group * rows), :]
            y = jnp.concatenate([y[g * rows : (g + 1) * rows] for g in range(group)], axis=1)
            z = jnp.dot(op, y, preferred_element_type=F32).astype(BF16)
            for g in range(group):
                for r in range(local):
                    z_s[pl.ds(pl.multiple_of(step * group * ROWS, group * ROWS) + g * ROWS, ROWS), r * wide : (r + 1) * wide] = z[
                        r * ROWS : (r + 1) * ROWS, g * wide : (g + 1) * wide
                    ]
            return carry

        lax.fori_loop(0, block // group, third, 0, unroll=2)
        half = local * wide // 2
        for part in range(2):
            got = jnp.dot(lk_s[...], z_s[:, part * half : (part + 1) * half], preferred_element_type=F32)
            out_ref[:, u, :, part * half : (part + 1) * half] = got.astype(BF16).reshape(sectors, block, half)
        return carry

    lax.fori_loop(0, local, last, 0)


def sigma_partial(live, labels, first, second, right, left, two, one, sectors, bond):
    block = first.shape[0]
    local = two.shape[0] // ROWS
    wide = 2 * block
    pair = local * local
    vmem = pl.BlockSpec(memory_space=pltpu.VMEM)
    return pl.pallas_call(
        functools.partial(sigma_kernel, block, bond, local),
        out_shape=jax.ShapeDtypeStruct((sectors, local, block, local * wide), BF16),
        in_specs=[pl.BlockSpec(memory_space=pltpu.SMEM)] + [vmem] * 7,
        out_specs=vmem,
        scratch_shapes=[
            pltpu.VMEM((pair * block, wide), BF16),
            pltpu.VMEM((bond * wide, wide), BF16),
            pltpu.VMEM((block * pair * ROWS, wide), F32),
            pltpu.VMEM((local, block * local * ROWS, wide), BF16),
            pltpu.VMEM((block * ROWS, local * wide), BF16),
            pltpu.VMEM((sectors * block, block * ROWS), BF16),
        ],
        compiler_params=pltpu.CompilerParams(vmem_limit_bytes=56 * 1024 * 1024),
    )(live, labels, first, second, right, left, two, one)


def shards(
    psi_first, psi_second, left_env, right_env, site_tensor, mpo, mpo_pattern, sector_labels, live_sizes,
):
    block_size = psi_first.shape[2]
    mpo_bond = mpo.shape[2]
    physical = site_tensor.shape[3] // block_size
    sectors = lax.axis_size("sector")
    kept = (jnp.arange(block_size, dtype=jnp.int32)[None, :] < live_sizes[0][:, None]).astype(BF16)
    masked = (mpo[0] * mpo_pattern[0][..., None].astype(BF16)).reshape(
        2, mpo_bond, mpo_bond, physical, physical
    )
    labels = sector_labels[0]
    one = padded_operator(masked[0], mpo_bond)
    two = padded_operator(masked[1], mpo_bond)
    left_t = jnp.pad(
        jnp.transpose(left_env[0, 0].reshape(block_size, mpo_bond, block_size), (0, 2, 1)),
        ((0, 0), (0, 0), (0, ROWS - mpo_bond)),
    ).reshape(block_size, block_size * ROWS)
    labels_row = jnp.tile(jnp.pad(labels[:, 0], (0, ROWS - mpo_bond), constant_values=-1), block_size)[None]
    partial = sigma_partial(
        live_sizes, labels_row, psi_first[0, 0], psi_second[0, 0], right_env[0, 0], left_t, two, one,
        sectors, mpo_bond,
    )
    site_part = (
        site_tensor[0].reshape(1, block_size, physical, block_size)
        * kept[:, :, None, None]
        * kept[:, None, None, :]
    )
    gathered = lax.all_gather(site_part, "sector", axis=0, tiled=True)
    left_part = left_env[0].reshape(1, block_size, mpo_bond, block_size)
    env_one = jnp.einsum("qbwa,qasc->qwbsc", left_part, site_part, preferred_element_type=F32).astype(BF16)
    bra = jnp.take(gathered, jnp.transpose(labels), axis=0)
    env_two = jnp.einsum("qwbre,qwbsc->qwresc", bra, env_one, preferred_element_type=F32).astype(BF16)
    updated = jnp.einsum("wvrs,qwresc->qevc", masked[0], env_two, preferred_element_type=F32).astype(BF16)
    updated = updated.reshape(1, 1, block_size, mpo_bond * block_size)
    count = lax.axis_size("chain")
    received = lax.ppermute(updated, "chain", [(i, i + 1) for i in range(count - 1)])
    next_env = jnp.where(lax.axis_index("chain") == 0, left_env, received)
    owned = lax.psum_scatter(partial, "sector", scatter_dimension=0, tiled=True)[0]
    owned = owned.reshape(physical, block_size, physical, 2, block_size).astype(F32)
    owned = owned * kept[0].astype(F32)[None, :, None, None, None] * kept[0].astype(F32)
    sigmas = jnp.transpose(owned, (3, 1, 2, 0, 4)).astype(BF16).reshape(2, 1, 1, block_size, -1)
    return (sigmas[0], sigmas[1], next_env)


def solution(mesh):
    return jax.shard_map(
        shards,
        mesh=mesh,
        in_specs=(
            P(("groups", "chain"), "sector", None, None),
            P(("groups", "chain"), "sector", None, None),
            P(("groups", "chain"), "sector", None, None),
            P(("groups", "chain"), "sector", None, None),
            P(("groups", "chain"), "sector", None, None),
            P(("groups", "chain"), None, None, None, None),
            P(("groups", "chain"), None, None, None),
            P(("groups", "chain"), None, "sector"),
            P(("groups", "chain"), "sector"),
        ),
        out_specs=(
            P(("groups", "chain"), "sector", None, None),
            P(("groups", "chain"), "sector", None, None),
            P(("groups", "chain"), "sector", None, None),
        ),
        check_vma=False,
    )
```

```python
import functools

import jax
import jax.numpy as jnp
from jax import lax
from jax.experimental import pallas as pl
from jax.experimental.pallas import tpu as pltpu
from jax.sharding import PartitionSpec as P

ROWS = 32
BF16 = jnp.bfloat16
F32 = jnp.float32
MESH = pl.DeviceIdType.MESH


def padded_operator(op, bond):
    op = jnp.transpose(op, (2, 0, 3, 1))
    op = jnp.pad(op, ((0, 0), (0, ROWS - bond), (0, 0), (0, ROWS - bond)))
    return op.reshape(op.shape[0] * ROWS, op.shape[2] * ROWS)


def window_kernel(
    block, bond, local, sectors, segments,
    live_ref, labels_ref, first_ref, second_ref, left_ref, right_ref, site_ref, left_t_ref, two_ref, one_ref,
    out_first_ref, out_second_ref, out_env_ref,
    psi_s, right_s, x_s, y_s, z_s, lk_s, site_s, site_t, v_s, sum_s, got_s, env_s, env_got,
    site_send, site_recv, sum_send, sum_recv, env_send, env_recv,
):
    me = lax.axis_index("sector")
    segment = lax.axis_index("chain")
    barrier = pltpu.get_barrier_semaphore()
    peers = [lax.rem(me + j, sectors) for j in range(1, sectors)]
    for peer in peers:
        pl.semaphore_signal(barrier, inc=1, device_id={"sector": peer}, device_id_type=MESH)

    @pl.when(segment > 0)
    def _():
        pl.semaphore_signal(barrier, inc=1, device_id={"chain": segment - 1}, device_id_type=MESH)

    @pl.when(segment < segments - 1)
    def _():
        pl.semaphore_signal(barrier, inc=1, device_id={"chain": segment + 1}, device_id_type=MESH)

    waits = sectors - 1 + jnp.where(segment > 0, 1, 0) + jnp.where(segment < segments - 1, 1, 0)
    pl.semaphore_wait(barrier, waits)

    wide = 2 * block
    pair = local * local
    live = live_ref[0, 0]
    low = lax.broadcasted_iota(jnp.int32, (block, local * block), 0) < live
    low = low & (lax.rem(lax.broadcasted_iota(jnp.int32, (block, local * block), 1), block) < live)
    site_s[me] = jnp.where(low, site_ref[...].astype(F32), 0.0).astype(BF16)

    def site_copy(j):
        return pltpu.make_async_remote_copy(
            src_ref=site_s.at[me], dst_ref=site_s.at[me], send_sem=site_send.at[j - 1],
            recv_sem=site_recv.at[j - 1], device_id={"sector": peers[j - 1]}, device_id_type=MESH,
        )

    for j in range(1, sectors):
        site_copy(j).start()
    row = lax.broadcasted_iota(jnp.int32, (block, wide), 0)
    lane = lax.broadcasted_iota(jnp.int32, (block, wide), 1)
    keep = (row < live) & (lax.rem(lane, block) < live)
    for tile in range(pair // 2):
        at = slice(tile * wide, (tile + 1) * wide)
        a = first_ref[:, at].astype(F32)
        b = second_ref[:, at].astype(F32)
        even = jnp.where(lane < block, a, pltpu.roll(b, block, 1))
        odd = jnp.where(lane < block, pltpu.roll(a, block, 1), b)
        psi_s[pl.ds(2 * tile * block, block), :] = jnp.where(keep, even, 0.0).astype(BF16)
        psi_s[pl.ds((2 * tile + 1) * block, block), :] = jnp.where(keep, odd, 0.0).astype(BF16)
    for tile in range(bond // 2):
        a = right_ref[:, tile * wide : (tile + 1) * wide].astype(F32)
        swapped = pltpu.roll(a, block, 1)
        zero = jnp.zeros_like(a)
        right_s[pl.ds(tile * 2 * wide, block), :] = jnp.where(lane < block, a, zero).astype(BF16)
        right_s[pl.ds(tile * 2 * wide + block, block), :] = jnp.where(lane < block, zero, swapped).astype(BF16)
        right_s[pl.ds(tile * 2 * wide + wide, block), :] = jnp.where(lane < block, swapped, zero).astype(BF16)
        right_s[pl.ds(tile * 2 * wide + wide + block, block), :] = jnp.where(lane < block, zero, a).astype(BF16)
    row_lane = lax.rem(lax.broadcasted_iota(jnp.int32, (block, wide), 1), ROWS)
    target = jnp.full((block, wide), -1, jnp.int32)
    for w in range(bond):
        target = jnp.where(row_lane == w, labels_ref[w, 0], target)
    for tile in range(block * ROWS // wide):
        at = slice(tile * wide, (tile + 1) * wide)
        a = left_t_ref[:, at].astype(F32)
        for k in range(sectors):
            lk_s[k * block : (k + 1) * block, at] = jnp.where(target == k, a, 0.0).astype(BF16)
    stride = pair * ROWS

    def put(st, w, value):
        x_s[pl.ds(st * ROWS + w, block, stride=stride), :] = value

    for st in range(pair):
        for w in range(bond, ROWS):
            put(st, w, jnp.zeros((block, wide), F32))

    def one(st, carry):
        lhs = psi_s[pl.ds(pl.multiple_of(st * block, block), block), :]
        for tile in range(bond // 2):
            got = lax.dot_general(
                lhs, right_s[pl.ds(tile * 2 * wide, 2 * wide), :], (((1,), (1,)), ((), ())),
                preferred_element_type=F32,
            )
            put(st, 2 * tile, got[:, :wide])
            put(st, 2 * tile + 1, got[:, wide:])
        return carry

    lax.fori_loop(0, pair, one, 0)
    two = two_ref[...]
    rows = local * ROWS

    def middle(a, carry):
        x = x_s[pl.ds(pl.multiple_of(a * stride, stride), stride), :].astype(BF16)
        x = jnp.concatenate([x[s * rows : (s + 1) * rows] for s in range(local)], axis=1)
        y = jnp.dot(two, x, preferred_element_type=F32).astype(BF16)
        for u in range(local):
            for s in range(local):
                y_s[u, pl.ds(pl.multiple_of(a * rows, rows) + s * ROWS, ROWS), :] = y[
                    u * ROWS : (u + 1) * ROWS, s * wide : (s + 1) * wide
                ]
        return carry

    lax.fori_loop(0, block, middle, 0, unroll=2)
    op = one_ref[...]
    group = 4

    def sum_copy(j, u):
        return pltpu.make_async_remote_copy(
            src_ref=sum_s.at[peers[j - 1], u], dst_ref=got_s.at[j - 1, u], send_sem=sum_send.at[j - 1, u],
            recv_sem=sum_recv.at[j - 1, u], device_id={"sector": peers[j - 1]}, device_id_type=MESH,
        )

    def last(u, carry):
        def third(step, carry):
            y = y_s[u, pl.ds(pl.multiple_of(step * group * rows, group * rows), group * rows), :]
            y = jnp.concatenate([y[g * rows : (g + 1) * rows] for g in range(group)], axis=1)
            z = jnp.dot(op, y, preferred_element_type=F32).astype(BF16)
            for g in range(group):
                for r in range(local):
                    z_s[pl.ds(pl.multiple_of(step * group * ROWS, group * ROWS) + g * ROWS, ROWS), r * wide : (r + 1) * wide] = z[
                        r * ROWS : (r + 1) * ROWS, g * wide : (g + 1) * wide
                    ]
            return carry

        lax.fori_loop(0, block // group, third, 0, unroll=2)
        half = local * wide // 2
        for part in range(2):
            got = jnp.dot(lk_s[...], z_s[:, part * half : (part + 1) * half], preferred_element_type=F32)
            sum_s[:, u, :, part * half : (part + 1) * half] = got.astype(BF16).reshape(sectors, block, half)
        for j in range(1, sectors):
            sum_copy(j, u).start()
        return carry

    lax.fori_loop(0, local, last, 0)

    for j in range(1, sectors):
        site_copy(j).wait()
    for q in range(sectors):
        site_t[q] = site_s[q].astype(F32).T.astype(BF16)
    own = site_s[me]
    own = jnp.concatenate([own, own], axis=0)
    op_t = op.astype(F32).T.astype(BF16)
    tiles = local * block // wide
    env_stride = tiles * rows

    def brought(tile, carry):
        a = left_ref[:, pl.ds(pl.multiple_of(tile * wide, wide), wide)].astype(F32)
        for odd in range(2):
            w = 2 * tile + odd
            part = jnp.where((lane >= block) if odd else (lane < block), a, 0.0).astype(BF16)
            e_one = jnp.dot(part, own, preferred_element_type=F32).astype(BF16)
            e_two = jnp.dot(site_t[labels_ref[w, 0]], e_one, preferred_element_type=F32)
            for t in range(tiles):
                for r in range(local):
                    x_s[pl.ds(t * rows + r * ROWS + w, block, stride=env_stride), :] = e_two[
                        r * block : (r + 1) * block, t * wide : (t + 1) * wide
                    ]
        return carry

    lax.fori_loop(0, bond // 2, brought, 0)

    def closed(e, carry):
        x = x_s[pl.ds(pl.multiple_of(e * env_stride, env_stride), env_stride), :].astype(BF16)
        x = jnp.concatenate([x[t * rows : (t + 1) * rows] for t in range(tiles)], axis=1)
        o = jnp.dot(op_t, x, preferred_element_type=F32)
        even = o[:ROWS, :wide]
        odd = o[ROWS : 2 * ROWS, :wide]
        for t in range(1, tiles):
            even = even + o[2 * t * ROWS : (2 * t + 1) * ROWS, t * wide : (t + 1) * wide]
            odd = odd + o[(2 * t + 1) * ROWS : (2 * t + 2) * ROWS, t * wide : (t + 1) * wide]
        v_s[pl.ds(e, ROWS, stride=block), :] = even + pltpu.roll(odd, block, 1)
        return carry

    lax.fori_loop(0, block, closed, 0, unroll=4)
    for tile in range(bond // 2):
        a = v_s[2 * tile * block : (2 * tile + 1) * block, :]
        b = v_s[(2 * tile + 1) * block : (2 * tile + 2) * block, :]
        env_s[:, tile * wide : (tile + 1) * wide] = jnp.where(lane < block, a, pltpu.roll(b, block, 1)).astype(BF16)

    def env_copy():
        return pltpu.make_async_remote_copy(
            src_ref=env_s, dst_ref=env_got, send_sem=env_send, recv_sem=env_recv,
            device_id={"chain": jnp.minimum(segment + 1, segments - 1)}, device_id_type=MESH,
        )

    @pl.when(segment < segments - 1)
    def _():
        env_copy().start()

    for u in range(0, local, 2):
        for j in range(1, sectors):
            sum_copy(j, u).wait()
            sum_copy(j, u + 1).wait()
        for r in range(local):
            at = slice(r * wide, (r + 1) * wide)
            total = []
            for v in range(2):
                t = sum_s[me, u + v, :, at].astype(F32)
                for j in range(sectors - 1):
                    t = t + got_s[j, u + v, :, at].astype(F32)
                total.append(jnp.where(keep, t, 0.0))
            a, b = total
            to = slice((r * local + u) * block, (r * local + u + 2) * block)
            out_first_ref[:, to] = jnp.where(lane < block, a, pltpu.roll(b, block, 1)).astype(BF16)
            out_second_ref[:, to] = jnp.where(lane < block, pltpu.roll(a, block, 1), b).astype(BF16)

    @pl.when(segment < segments - 1)
    def _():
        env_copy().wait_send()

    @pl.when(segment > 0)
    def _():
        env_copy().wait_recv()
        out_env_ref[...] = env_got[...]

    @pl.when(segment == 0)
    def _():
        out_env_ref[...] = left_ref[...]


def shards(
    psi_first, psi_second, left_env, right_env, site_tensor, mpo, mpo_pattern, sector_labels, live_sizes,
):
    block = psi_first.shape[2]
    bond = mpo.shape[2]
    local = site_tensor.shape[3] // block
    sectors = lax.axis_size("sector")
    segments = lax.axis_size("chain")
    wide = 2 * block
    pair = local * local
    masked = (mpo[0] * mpo_pattern[0][..., None].astype(BF16)).reshape(2, bond, bond, local, local)
    one = padded_operator(masked[0], bond)
    two = padded_operator(masked[1], bond)
    left = left_env[0, 0]
    left_t = jnp.pad(
        jnp.transpose(left.reshape(block, bond, block), (0, 2, 1)), ((0, 0), (0, 0), (0, ROWS - bond))
    ).reshape(block, block * ROWS)
    vmem = pl.BlockSpec(memory_space=pltpu.VMEM)
    smem = pl.BlockSpec(memory_space=pltpu.SMEM)
    outs = pl.pallas_call(
        functools.partial(window_kernel, block, bond, local, sectors, segments),
        out_shape=(
            jax.ShapeDtypeStruct((block, pair * block), BF16),
            jax.ShapeDtypeStruct((block, pair * block), BF16),
            jax.ShapeDtypeStruct((block, bond * block), BF16),
        ),
        in_specs=[smem] * 2 + [vmem] * 8,
        out_specs=(vmem,) * 3,
        scratch_shapes=[
            pltpu.VMEM((pair * block, wide), BF16),
            pltpu.VMEM((bond * wide, wide), BF16),
            pltpu.VMEM((block * pair * ROWS, wide), F32),
            pltpu.VMEM((local, block * local * ROWS, wide), BF16),
            pltpu.VMEM((block * ROWS, local * wide), BF16),
            pltpu.VMEM((sectors * block, block * ROWS), BF16),
            pltpu.VMEM((sectors, block, local * block), BF16),
            pltpu.VMEM((sectors, local * block, block), BF16),
            pltpu.VMEM((ROWS * block, wide), F32),
            pltpu.VMEM((sectors, local, block, local * wide), BF16),
            pltpu.VMEM((sectors - 1, local, block, local * wide), BF16),
            pltpu.VMEM((block, bond * block), BF16),
            pltpu.VMEM((block, bond * block), BF16),
            pltpu.SemaphoreType.DMA((sectors - 1,)),
            pltpu.SemaphoreType.DMA((sectors - 1,)),
            pltpu.SemaphoreType.DMA((sectors - 1, local)),
            pltpu.SemaphoreType.DMA((sectors - 1, local)),
            pltpu.SemaphoreType.DMA,
            pltpu.SemaphoreType.DMA,
        ],
        compiler_params=pltpu.CompilerParams(
            vmem_limit_bytes=56 * 1024 * 1024, collective_id=0, has_side_effects=True
        ),
    )(
        live_sizes, sector_labels[0], psi_first[0, 0], psi_second[0, 0], left, right_env[0, 0],
        site_tensor[0, 0], left_t, two, one,
    )
    return tuple(out[None, None] for out in outs)


def solution(mesh):
    return jax.shard_map(
        shards,
        mesh=mesh,
        in_specs=(
            P(("groups", "chain"), "sector", None, None),
            P(("groups", "chain"), "sector", None, None),
            P(("groups", "chain"), "sector", None, None),
            P(("groups", "chain"), "sector", None, None),
            P(("groups", "chain"), "sector", None, None),
            P(("groups", "chain"), None, None, None, None),
            P(("groups", "chain"), None, None, None),
            P(("groups", "chain"), None, "sector"),
            P(("groups", "chain"), "sector"),
        ),
        out_specs=(
            P(("groups", "chain"), "sector", None, None),
            P(("groups", "chain"), "sector", None, None),
            P(("groups", "chain"), "sector", None, None),
        ),
        check_vma=False,
    )
```

```python
import functools

import jax
import jax.numpy as jnp
from jax import lax
from jax.experimental import pallas as pl
from jax.experimental.pallas import tpu as pltpu
from jax.sharding import PartitionSpec as P

ROWS = 32
SKEW = 8
BF16 = jnp.bfloat16
F32 = jnp.float32
MESH = pl.DeviceIdType.MESH


def padded_operator(op, bond):
    op = jnp.transpose(op, (2, 0, 3, 1))
    op = jnp.pad(op, ((0, 0), (0, ROWS - bond), (0, 0), (0, ROWS - bond)))
    return op.reshape(op.shape[0] * ROWS, op.shape[2] * ROWS)


def window_kernel(
    block, bond, local, sectors, segments,
    live_ref, labels_ref, first_ref, second_ref, left_ref, right_ref, site_ref, left_t_ref, two_ref, one_ref,
    out_first_ref, out_second_ref, out_env_ref,
    psi_s, right_s, x_s, y_s, z_s, lk_s, site_s, site_t, v_s, sum_s, got_s, env_s, env_got,
    site_send, site_recv, sum_send, sum_recv, env_send, env_recv,
):
    me = lax.axis_index("sector")
    segment = lax.axis_index("chain")
    barrier = pltpu.get_barrier_semaphore()
    peers = [lax.rem(me + j, sectors) for j in range(1, sectors)]
    for peer in peers:
        pl.semaphore_signal(barrier, inc=1, device_id={"sector": peer}, device_id_type=MESH)

    @pl.when(segment > 0)
    def _():
        pl.semaphore_signal(barrier, inc=1, device_id={"chain": segment - 1}, device_id_type=MESH)

    @pl.when(segment < segments - 1)
    def _():
        pl.semaphore_signal(barrier, inc=1, device_id={"chain": segment + 1}, device_id_type=MESH)

    waits = sectors - 1 + jnp.where(segment > 0, 1, 0) + jnp.where(segment < segments - 1, 1, 0)
    pl.semaphore_wait(barrier, waits)

    wide = 2 * block
    pair = local * local
    live = live_ref[0, 0]
    low = lax.broadcasted_iota(jnp.int32, (block, local * block), 0) < live
    low = low & (lax.rem(lax.broadcasted_iota(jnp.int32, (block, local * block), 1), block) < live)
    site_s[me] = jnp.where(low, site_ref[...].astype(F32), 0.0).astype(BF16)

    def site_copy(j):
        return pltpu.make_async_remote_copy(
            src_ref=site_s.at[me], dst_ref=site_s.at[me], send_sem=site_send.at[j - 1],
            recv_sem=site_recv.at[j - 1], device_id={"sector": peers[j - 1]}, device_id_type=MESH,
        )

    for j in range(1, sectors):
        site_copy(j).start()
    row = lax.broadcasted_iota(jnp.int32, (block, wide), 0)
    lane = lax.broadcasted_iota(jnp.int32, (block, wide), 1)
    keep = (row < live) & (lax.rem(lane, block) < live)
    for tile in range(pair // 2):
        at = slice(tile * wide, (tile + 1) * wide)
        a = first_ref[:, at].astype(F32)
        b = second_ref[:, at].astype(F32)
        even = jnp.where(lane < block, a, pltpu.roll(b, block, 1))
        odd = jnp.where(lane < block, pltpu.roll(a, block, 1), b)
        psi_s[pl.ds(2 * tile * block, block), :] = jnp.where(keep, even, 0.0).astype(BF16)
        psi_s[pl.ds((2 * tile + 1) * block, block), :] = jnp.where(keep, odd, 0.0).astype(BF16)
    for tile in range(bond // 2):
        a = right_ref[:, tile * wide : (tile + 1) * wide].astype(F32)
        swapped = pltpu.roll(a, block, 1)
        zero = jnp.zeros_like(a)
        right_s[pl.ds(tile * 2 * wide, block), :] = jnp.where(lane < block, a, zero).astype(BF16)
        right_s[pl.ds(tile * 2 * wide + block, block), :] = jnp.where(lane < block, zero, swapped).astype(BF16)
        right_s[pl.ds(tile * 2 * wide + wide, block), :] = jnp.where(lane < block, swapped, zero).astype(BF16)
        right_s[pl.ds(tile * 2 * wide + wide + block, block), :] = jnp.where(lane < block, zero, a).astype(BF16)
    row_lane = lax.rem(lax.broadcasted_iota(jnp.int32, (block, wide), 1), ROWS)
    target = jnp.full((block, wide), -1, jnp.int32)
    for w in range(bond):
        target = jnp.where(row_lane == w, labels_ref[w, 0], target)
    for tile in range(block * ROWS // wide):
        at = slice(tile * wide, (tile + 1) * wide)
        a = left_t_ref[:, at].astype(F32)
        for k in range(sectors):
            lk_s[k * block : (k + 1) * block, at] = jnp.where(target == k, a, 0.0).astype(BF16)
    stride = pair * ROWS + SKEW

    def put(st, w, value):
        x_s[pl.ds(st * ROWS + w, block, stride=stride), :] = value

    for a in range(block):
        x_s[pl.ds(a * stride + pair * ROWS, SKEW), :] = jnp.zeros((SKEW, wide), F32)
    for st in range(pair):
        for w in range(bond, ROWS):
            put(st, w, jnp.zeros((block, wide), F32))

    together = 4
    for tile in range(bond // 2):
        rhs = right_s[pl.ds(tile * 2 * wide, 2 * wide), :]
        for st in range(0, pair, together):
            got = lax.dot_general(
                psi_s[pl.ds(st * block, together * block), :], rhs, (((1,), (1,)), ((), ())),
                preferred_element_type=F32,
            )
            for i in range(together):
                put(st + i, 2 * tile, got[i * block : (i + 1) * block, :wide])
                put(st + i, 2 * tile + 1, got[i * block : (i + 1) * block, wide:])

    two = two_ref[...]
    rows = local * ROWS

    def middle(a, carry):
        x = x_s[pl.ds(pl.multiple_of(a * stride, SKEW), pair * ROWS), :].astype(BF16)
        x = jnp.concatenate([x[s * rows : (s + 1) * rows] for s in range(local)], axis=1)
        y = jnp.dot(two, x, preferred_element_type=F32).astype(BF16)
        for u in range(local):
            for s in range(local):
                y_s[u, pl.ds(pl.multiple_of(a * rows, rows) + s * ROWS, ROWS), :] = y[
                    u * ROWS : (u + 1) * ROWS, s * wide : (s + 1) * wide
                ]
        return carry

    lax.fori_loop(0, block, middle, 0, unroll=2)
    op = one_ref[...]
    group = 4

    def sum_copy(j, u):
        return pltpu.make_async_remote_copy(
            src_ref=sum_s.at[peers[j - 1], u], dst_ref=got_s.at[j - 1, u], send_sem=sum_send.at[j - 1, u],
            recv_sem=sum_recv.at[j - 1, u], device_id={"sector": peers[j - 1]}, device_id_type=MESH,
        )

    def last(u, carry):
        def third(step, carry):
            y = y_s[u, pl.ds(pl.multiple_of(step * group * rows, group * rows), group * rows), :]
            y = jnp.concatenate([y[g * rows : (g + 1) * rows] for g in range(group)], axis=1)
            z = jnp.dot(op, y, preferred_element_type=F32).astype(BF16)
            for g in range(group):
                for r in range(local):
                    z_s[pl.ds(pl.multiple_of(step * group * ROWS, group * ROWS) + g * ROWS, ROWS), r * wide : (r + 1) * wide] = z[
                        r * ROWS : (r + 1) * ROWS, g * wide : (g + 1) * wide
                    ]
            return carry

        lax.fori_loop(0, block // group, third, 0, unroll=2)
        half = local * wide // 2
        for part in range(2):
            got = jnp.dot(lk_s[...], z_s[:, part * half : (part + 1) * half], preferred_element_type=F32)
            sum_s[:, u, :, part * half : (part + 1) * half] = got.astype(BF16).reshape(sectors, block, half)
        for j in range(1, sectors):
            sum_copy(j, u).start()
        return carry

    lax.fori_loop(0, local, last, 0)

    for j in range(1, sectors):
        site_copy(j).wait()
    for q in range(sectors):
        site_t[q] = site_s[q].astype(F32).T.astype(BF16)
    own = site_s[me]
    own = jnp.concatenate([own, own], axis=0)
    op_t = op.astype(F32).T.astype(BF16)
    tiles = local * block // wide
    env_stride = tiles * rows + SKEW

    def brought(tile, carry):
        a = left_ref[:, pl.ds(pl.multiple_of(tile * wide, wide), wide)].astype(F32)
        for odd in range(2):
            w = 2 * tile + odd
            part = jnp.where((lane >= block) if odd else (lane < block), a, 0.0).astype(BF16)
            e_one = jnp.dot(part, own, preferred_element_type=F32).astype(BF16)
            e_two = jnp.dot(site_t[labels_ref[w, 0]], e_one, preferred_element_type=F32)
            for t in range(tiles):
                for r in range(local):
                    x_s[pl.ds(t * rows + r * ROWS + w, block, stride=env_stride), :] = e_two[
                        r * block : (r + 1) * block, t * wide : (t + 1) * wide
                    ]
        return carry

    lax.fori_loop(0, bond // 2, brought, 0)

    def closed(e, carry):
        x = x_s[pl.ds(pl.multiple_of(e * env_stride, SKEW), tiles * rows), :].astype(BF16)
        x = jnp.concatenate([x[t * rows : (t + 1) * rows] for t in range(tiles)], axis=1)
        o = jnp.dot(op_t, x, preferred_element_type=F32)
        even = o[:ROWS, :wide]
        odd = o[ROWS : 2 * ROWS, :wide]
        for t in range(1, tiles):
            even = even + o[2 * t * ROWS : (2 * t + 1) * ROWS, t * wide : (t + 1) * wide]
            odd = odd + o[(2 * t + 1) * ROWS : (2 * t + 2) * ROWS, t * wide : (t + 1) * wide]
        v_s[pl.ds(e, ROWS, stride=block), :] = even + pltpu.roll(odd, block, 1)
        return carry

    lax.fori_loop(0, block, closed, 0, unroll=4)
    for tile in range(bond // 2):
        a = v_s[2 * tile * block : (2 * tile + 1) * block, :]
        b = v_s[(2 * tile + 1) * block : (2 * tile + 2) * block, :]
        env_s[:, tile * wide : (tile + 1) * wide] = jnp.where(lane < block, a, pltpu.roll(b, block, 1)).astype(BF16)

    def env_copy():
        return pltpu.make_async_remote_copy(
            src_ref=env_s, dst_ref=env_got, send_sem=env_send, recv_sem=env_recv,
            device_id={"chain": jnp.minimum(segment + 1, segments - 1)}, device_id_type=MESH,
        )

    @pl.when(segment < segments - 1)
    def _():
        env_copy().start()

    for u in range(0, local, 2):
        for j in range(1, sectors):
            sum_copy(j, u).wait()
            sum_copy(j, u + 1).wait()
        for r in range(local):
            at = slice(r * wide, (r + 1) * wide)
            total = []
            for v in range(2):
                t = sum_s[me, u + v, :, at].astype(F32)
                for j in range(sectors - 1):
                    t = t + got_s[j, u + v, :, at].astype(F32)
                total.append(jnp.where(keep, t, 0.0))
            a, b = total
            to = slice((r * local + u) * block, (r * local + u + 2) * block)
            out_first_ref[:, to] = jnp.where(lane < block, a, pltpu.roll(b, block, 1)).astype(BF16)
            out_second_ref[:, to] = jnp.where(lane < block, pltpu.roll(a, block, 1), b).astype(BF16)

    @pl.when(segment < segments - 1)
    def _():
        env_copy().wait_send()

    @pl.when(segment > 0)
    def _():
        env_copy().wait_recv()
        out_env_ref[...] = env_got[...]

    @pl.when(segment == 0)
    def _():
        out_env_ref[...] = left_ref[...]


def shards(
    psi_first, psi_second, left_env, right_env, site_tensor, mpo, mpo_pattern, sector_labels, live_sizes,
):
    block = psi_first.shape[2]
    bond = mpo.shape[2]
    local = site_tensor.shape[3] // block
    sectors = lax.axis_size("sector")
    segments = lax.axis_size("chain")
    wide = 2 * block
    pair = local * local
    masked = (mpo[0] * mpo_pattern[0][..., None].astype(BF16)).reshape(2, bond, bond, local, local)
    one = padded_operator(masked[0], bond)
    two = padded_operator(masked[1], bond)
    left = left_env[0, 0]
    left_t = jnp.pad(
        jnp.transpose(left.reshape(block, bond, block), (0, 2, 1)), ((0, 0), (0, 0), (0, ROWS - bond))
    ).reshape(block, block * ROWS)
    vmem = pl.BlockSpec(memory_space=pltpu.VMEM)
    smem = pl.BlockSpec(memory_space=pltpu.SMEM)
    outs = pl.pallas_call(
        functools.partial(window_kernel, block, bond, local, sectors, segments),
        out_shape=(
            jax.ShapeDtypeStruct((block, pair * block), BF16),
            jax.ShapeDtypeStruct((block, pair * block), BF16),
            jax.ShapeDtypeStruct((block, bond * block), BF16),
        ),
        in_specs=[smem] * 2 + [vmem] * 8,
        out_specs=(vmem,) * 3,
        scratch_shapes=[
            pltpu.VMEM((pair * block, wide), BF16),
            pltpu.VMEM((bond * wide, wide), BF16),
            pltpu.VMEM((block * (pair * ROWS + SKEW), wide), F32),
            pltpu.VMEM((local, block * local * ROWS, wide), BF16),
            pltpu.VMEM((block * ROWS, local * wide), BF16),
            pltpu.VMEM((sectors * block, block * ROWS), BF16),
            pltpu.VMEM((sectors, block, local * block), BF16),
            pltpu.VMEM((sectors, local * block, block), BF16),
            pltpu.VMEM((ROWS * block, wide), F32),
            pltpu.VMEM((sectors, local, block, local * wide), BF16),
            pltpu.VMEM((sectors - 1, local, block, local * wide), BF16),
            pltpu.VMEM((block, bond * block), BF16),
            pltpu.VMEM((block, bond * block), BF16),
            pltpu.SemaphoreType.DMA((sectors - 1,)),
            pltpu.SemaphoreType.DMA((sectors - 1,)),
            pltpu.SemaphoreType.DMA((sectors - 1, local)),
            pltpu.SemaphoreType.DMA((sectors - 1, local)),
            pltpu.SemaphoreType.DMA,
            pltpu.SemaphoreType.DMA,
        ],
        compiler_params=pltpu.CompilerParams(
            vmem_limit_bytes=56 * 1024 * 1024, collective_id=0, has_side_effects=True
        ),
    )(
        live_sizes, sector_labels[0], psi_first[0, 0], psi_second[0, 0], left, right_env[0, 0],
        site_tensor[0, 0], left_t, two, one,
    )
    return tuple(out[None, None] for out in outs)


def solution(mesh):
    return jax.shard_map(
        shards,
        mesh=mesh,
        in_specs=(
            P(("groups", "chain"), "sector", None, None),
            P(("groups", "chain"), "sector", None, None),
            P(("groups", "chain"), "sector", None, None),
            P(("groups", "chain"), "sector", None, None),
            P(("groups", "chain"), "sector", None, None),
            P(("groups", "chain"), None, None, None, None),
            P(("groups", "chain"), None, None, None),
            P(("groups", "chain"), None, "sector"),
            P(("groups", "chain"), "sector"),
        ),
        out_specs=(
            P(("groups", "chain"), "sector", None, None),
            P(("groups", "chain"), "sector", None, None),
            P(("groups", "chain"), "sector", None, None),
        ),
        check_vma=False,
    )
```

```python
import functools

import jax
import jax.numpy as jnp
from jax import lax
from jax.experimental import pallas as pl
from jax.experimental.pallas import tpu as pltpu
from jax.sharding import PartitionSpec as P

ROWS = 32
SKEW = 9
BF16 = jnp.bfloat16
F32 = jnp.float32
MESH = pl.DeviceIdType.MESH


def padded_operator(op, bond):
    op = jnp.transpose(op, (2, 0, 3, 1))
    op = jnp.pad(op, ((0, 0), (0, ROWS - bond), (0, 0), (0, ROWS - bond)))
    return op.reshape(op.shape[0] * ROWS, op.shape[2] * ROWS)


def window_kernel(
    block, bond, local, sectors, segments,
    live_ref, labels_ref, first_ref, second_ref, left_ref, right_ref, site_ref, left_t_ref, two_ref, one_ref,
    out_first_ref, out_second_ref, out_env_ref,
    psi_s, right_s, x_s, y_s, z_s, lk_s, site_s, site_t, v_s, sum_s, got_s, env_s, env_got,
    site_send, site_recv, sum_send, sum_recv, env_send, env_recv,
):
    me = lax.axis_index("sector")
    segment = lax.axis_index("chain")
    barrier = pltpu.get_barrier_semaphore()
    peers = [lax.rem(me + j, sectors) for j in range(1, sectors)]
    for peer in peers:
        pl.semaphore_signal(barrier, inc=1, device_id={"sector": peer}, device_id_type=MESH)

    @pl.when(segment > 0)
    def _():
        pl.semaphore_signal(barrier, inc=1, device_id={"chain": segment - 1}, device_id_type=MESH)

    @pl.when(segment < segments - 1)
    def _():
        pl.semaphore_signal(barrier, inc=1, device_id={"chain": segment + 1}, device_id_type=MESH)

    waits = sectors - 1 + jnp.where(segment > 0, 1, 0) + jnp.where(segment < segments - 1, 1, 0)
    pl.semaphore_wait(barrier, waits)

    wide = 2 * block
    pair = local * local
    live = live_ref[0, 0]
    low = lax.broadcasted_iota(jnp.int32, (block, local * block), 0) < live
    low = low & (lax.rem(lax.broadcasted_iota(jnp.int32, (block, local * block), 1), block) < live)
    site_s[me] = jnp.where(low, site_ref[...].astype(F32), 0.0).astype(BF16)

    def site_copy(j):
        return pltpu.make_async_remote_copy(
            src_ref=site_s.at[me], dst_ref=site_s.at[me], send_sem=site_send.at[j - 1],
            recv_sem=site_recv.at[j - 1], device_id={"sector": peers[j - 1]}, device_id_type=MESH,
        )

    for j in range(1, sectors):
        site_copy(j).start()
    row = lax.broadcasted_iota(jnp.int32, (block, wide), 0)
    lane = lax.broadcasted_iota(jnp.int32, (block, wide), 1)
    keep = (row < live) & (lax.rem(lane, block) < live)
    for tile in range(pair // 2):
        at = slice(tile * wide, (tile + 1) * wide)
        a = first_ref[:, at].astype(F32)
        b = second_ref[:, at].astype(F32)
        even = jnp.where(lane < block, a, pltpu.roll(b, block, 1))
        odd = jnp.where(lane < block, pltpu.roll(a, block, 1), b)
        psi_s[pl.ds(2 * tile * block, block), :] = jnp.where(keep, even, 0.0).astype(BF16)
        psi_s[pl.ds((2 * tile + 1) * block, block), :] = jnp.where(keep, odd, 0.0).astype(BF16)
    for tile in range(bond // 2):
        a = right_ref[:, tile * wide : (tile + 1) * wide].astype(F32)
        swapped = pltpu.roll(a, block, 1)
        zero = jnp.zeros_like(a)
        right_s[pl.ds(tile * 2 * wide, block), :] = jnp.where(lane < block, a, zero).astype(BF16)
        right_s[pl.ds(tile * 2 * wide + block, block), :] = jnp.where(lane < block, zero, swapped).astype(BF16)
        right_s[pl.ds(tile * 2 * wide + wide, block), :] = jnp.where(lane < block, swapped, zero).astype(BF16)
        right_s[pl.ds(tile * 2 * wide + wide + block, block), :] = jnp.where(lane < block, zero, a).astype(BF16)
    row_lane = lax.rem(lax.broadcasted_iota(jnp.int32, (block, wide), 1), ROWS)
    target = jnp.full((block, wide), -1, jnp.int32)
    for w in range(bond):
        target = jnp.where(row_lane == w, labels_ref[w, 0], target)
    for tile in range(block * ROWS // wide):
        at = slice(tile * wide, (tile + 1) * wide)
        a = left_t_ref[:, at].astype(F32)
        for k in range(sectors):
            lk_s[k * block : (k + 1) * block, at] = jnp.where(target == k, a, 0.0).astype(BF16)
    stride = pair * ROWS + SKEW

    def put(st, w, value):
        x_s[pl.ds(st * ROWS + w, block, stride=stride), :] = value

    for a in range(block):
        x_s[pl.ds(a * stride + pair * ROWS, SKEW), :] = jnp.zeros((SKEW, wide), F32)
    for st in range(pair):
        for w in range(bond, ROWS):
            put(st, w, jnp.zeros((block, wide), F32))

    together = 4
    for tile in range(bond // 2):
        rhs = right_s[pl.ds(tile * 2 * wide, 2 * wide), :]
        for st in range(0, pair, together):
            got = lax.dot_general(
                psi_s[pl.ds(st * block, together * block), :], rhs, (((1,), (1,)), ((), ())),
                preferred_element_type=F32,
            )
            for i in range(together):
                put(st + i, 2 * tile, got[i * block : (i + 1) * block, :wide])
                put(st + i, 2 * tile + 1, got[i * block : (i + 1) * block, wide:])

    two = two_ref[...]
    rows = local * ROWS

    def middle(a, carry):
        x = x_s[pl.ds(a * stride, pair * ROWS), :].astype(BF16)
        x = jnp.concatenate([x[s * rows : (s + 1) * rows] for s in range(local)], axis=1)
        y = jnp.dot(two, x, preferred_element_type=F32).astype(BF16)
        for u in range(local):
            for s in range(local):
                y_s[u, pl.ds(pl.multiple_of(a * rows, rows) + s * ROWS, ROWS), :] = y[
                    u * ROWS : (u + 1) * ROWS, s * wide : (s + 1) * wide
                ]
        return carry

    lax.fori_loop(0, block, middle, 0, unroll=4)
    op = one_ref[...]
    group = 8

    def sum_copy(j, u):
        return pltpu.make_async_remote_copy(
            src_ref=sum_s.at[peers[j - 1], u], dst_ref=got_s.at[j - 1, u], send_sem=sum_send.at[j - 1, u],
            recv_sem=sum_recv.at[j - 1, u], device_id={"sector": peers[j - 1]}, device_id_type=MESH,
        )

    def last(u, carry):
        def third(step, carry):
            y = y_s[u, pl.ds(pl.multiple_of(step * group * rows, group * rows), group * rows), :]
            y = jnp.concatenate([y[g * rows : (g + 1) * rows] for g in range(group)], axis=1)
            z = jnp.dot(op, y, preferred_element_type=F32).astype(BF16)
            for g in range(group):
                for r in range(local):
                    z_s[pl.ds(pl.multiple_of(step * group * ROWS, group * ROWS) + g * ROWS, ROWS), r * wide : (r + 1) * wide] = z[
                        r * ROWS : (r + 1) * ROWS, g * wide : (g + 1) * wide
                    ]
            return carry

        lax.fori_loop(0, block // group, third, 0, unroll=2)
        half = local * wide // 2
        for part in range(2):
            got = jnp.dot(lk_s[...], z_s[:, part * half : (part + 1) * half], preferred_element_type=F32)
            sum_s[:, u, :, part * half : (part + 1) * half] = got.astype(BF16).reshape(sectors, block, half)
        for j in range(1, sectors):
            sum_copy(j, u).start()
        return carry

    lax.fori_loop(0, local, last, 0)

    for j in range(1, sectors):
        site_copy(j).wait()
    for q in range(sectors):
        site_t[q] = site_s[q].astype(F32).T.astype(BF16)
    own = site_s[me]
    own = jnp.concatenate([own, own], axis=0)
    op_t = op.astype(F32).T.astype(BF16)
    tiles = local * block // wide
    env_stride = tiles * rows + SKEW

    def brought(tile, carry):
        a = left_ref[:, pl.ds(pl.multiple_of(tile * wide, wide), wide)].astype(F32)
        for odd in range(2):
            w = 2 * tile + odd
            part = jnp.where((lane >= block) if odd else (lane < block), a, 0.0).astype(BF16)
            e_one = jnp.dot(part, own, preferred_element_type=F32).astype(BF16)
            e_two = jnp.dot(site_t[labels_ref[w, 0]], e_one, preferred_element_type=F32)
            for t in range(tiles):
                for r in range(local):
                    x_s[pl.ds(t * rows + r * ROWS + w, block, stride=env_stride), :] = e_two[
                        r * block : (r + 1) * block, t * wide : (t + 1) * wide
                    ]
        return carry

    lax.fori_loop(0, bond // 2, brought, 0, unroll=True)

    def closed(e, carry):
        x = x_s[pl.ds(e * env_stride, tiles * rows), :].astype(BF16)
        x = jnp.concatenate([x[t * rows : (t + 1) * rows] for t in range(tiles)], axis=1)
        o = jnp.dot(op_t, x, preferred_element_type=F32)
        even = o[:ROWS, :wide]
        odd = o[ROWS : 2 * ROWS, :wide]
        for t in range(1, tiles):
            even = even + o[2 * t * ROWS : (2 * t + 1) * ROWS, t * wide : (t + 1) * wide]
            odd = odd + o[(2 * t + 1) * ROWS : (2 * t + 2) * ROWS, t * wide : (t + 1) * wide]
        v_s[pl.ds(e, ROWS, stride=block), :] = even + pltpu.roll(odd, block, 1)
        return carry

    lax.fori_loop(0, block, closed, 0, unroll=4)
    for tile in range(bond // 2):
        a = v_s[2 * tile * block : (2 * tile + 1) * block, :]
        b = v_s[(2 * tile + 1) * block : (2 * tile + 2) * block, :]
        env_s[:, tile * wide : (tile + 1) * wide] = jnp.where(lane < block, a, pltpu.roll(b, block, 1)).astype(BF16)

    def env_copy():
        return pltpu.make_async_remote_copy(
            src_ref=env_s, dst_ref=env_got, send_sem=env_send, recv_sem=env_recv,
            device_id={"chain": jnp.minimum(segment + 1, segments - 1)}, device_id_type=MESH,
        )

    @pl.when(segment < segments - 1)
    def _():
        env_copy().start()

    for u in range(0, local, 2):
        for j in range(1, sectors):
            sum_copy(j, u).wait()
            sum_copy(j, u + 1).wait()
        for r in range(local):
            at = slice(r * wide, (r + 1) * wide)
            total = []
            for v in range(2):
                t = sum_s[me, u + v, :, at].astype(F32)
                for j in range(sectors - 1):
                    t = t + got_s[j, u + v, :, at].astype(F32)
                total.append(jnp.where(keep, t, 0.0))
            a, b = total
            to = slice((r * local + u) * block, (r * local + u + 2) * block)
            out_first_ref[:, to] = jnp.where(lane < block, a, pltpu.roll(b, block, 1)).astype(BF16)
            out_second_ref[:, to] = jnp.where(lane < block, pltpu.roll(a, block, 1), b).astype(BF16)

    @pl.when(segment < segments - 1)
    def _():
        env_copy().wait_send()

    @pl.when(segment > 0)
    def _():
        env_copy().wait_recv()
        out_env_ref[...] = env_got[...]

    @pl.when(segment == 0)
    def _():
        out_env_ref[...] = left_ref[...]


def shards(
    psi_first, psi_second, left_env, right_env, site_tensor, mpo, mpo_pattern, sector_labels, live_sizes,
):
    block = psi_first.shape[2]
    bond = mpo.shape[2]
    local = site_tensor.shape[3] // block
    sectors = lax.axis_size("sector")
    segments = lax.axis_size("chain")
    wide = 2 * block
    pair = local * local
    masked = (mpo[0] * mpo_pattern[0][..., None].astype(BF16)).reshape(2, bond, bond, local, local)
    one = padded_operator(masked[0], bond)
    two = padded_operator(masked[1], bond)
    left = left_env[0, 0]
    left_t = jnp.pad(
        jnp.transpose(left.reshape(block, bond, block), (0, 2, 1)), ((0, 0), (0, 0), (0, ROWS - bond))
    ).reshape(block, block * ROWS)
    vmem = pl.BlockSpec(memory_space=pltpu.VMEM)
    smem = pl.BlockSpec(memory_space=pltpu.SMEM)
    outs = pl.pallas_call(
        functools.partial(window_kernel, block, bond, local, sectors, segments),
        out_shape=(
            jax.ShapeDtypeStruct((block, pair * block), BF16),
            jax.ShapeDtypeStruct((block, pair * block), BF16),
            jax.ShapeDtypeStruct((block, bond * block), BF16),
        ),
        in_specs=[smem] * 2 + [vmem] * 8,
        out_specs=(vmem,) * 3,
        scratch_shapes=[
            pltpu.VMEM((pair * block, wide), BF16),
            pltpu.VMEM((bond * wide, wide), BF16),
            pltpu.VMEM((block * (pair * ROWS + SKEW), wide), F32),
            pltpu.VMEM((local, block * local * ROWS, wide), BF16),
            pltpu.VMEM((block * ROWS, local * wide), BF16),
            pltpu.VMEM((sectors * block, block * ROWS), BF16),
            pltpu.VMEM((sectors, block, local * block), BF16),
            pltpu.VMEM((sectors, local * block, block), BF16),
            pltpu.VMEM((ROWS * block, wide), F32),
            pltpu.VMEM((sectors, local, block, local * wide), BF16),
            pltpu.VMEM((sectors - 1, local, block, local * wide), BF16),
            pltpu.VMEM((block, bond * block), BF16),
            pltpu.VMEM((block, bond * block), BF16),
            pltpu.SemaphoreType.DMA((sectors - 1,)),
            pltpu.SemaphoreType.DMA((sectors - 1,)),
            pltpu.SemaphoreType.DMA((sectors - 1, local)),
            pltpu.SemaphoreType.DMA((sectors - 1, local)),
            pltpu.SemaphoreType.DMA,
            pltpu.SemaphoreType.DMA,
        ],
        compiler_params=pltpu.CompilerParams(
            vmem_limit_bytes=56 * 1024 * 1024, collective_id=0, has_side_effects=True
        ),
    )(
        live_sizes, sector_labels[0], psi_first[0, 0], psi_second[0, 0], left, right_env[0, 0],
        site_tensor[0, 0], left_t, two, one,
    )
    return tuple(out[None, None] for out in outs)


def solution(mesh):
    return jax.shard_map(
        shards,
        mesh=mesh,
        in_specs=(
            P(("groups", "chain"), "sector", None, None),
            P(("groups", "chain"), "sector", None, None),
            P(("groups", "chain"), "sector", None, None),
            P(("groups", "chain"), "sector", None, None),
            P(("groups", "chain"), "sector", None, None),
            P(("groups", "chain"), None, None, None, None),
            P(("groups", "chain"), None, None, None),
            P(("groups", "chain"), None, "sector"),
            P(("groups", "chain"), "sector"),
        ),
        out_specs=(
            P(("groups", "chain"), "sector", None, None),
            P(("groups", "chain"), "sector", None, None),
            P(("groups", "chain"), "sector", None, None),
        ),
        check_vma=False,
    )
```
